32 devices in a mesh: dp: 4 (over y, core), seq: 8 (over z, x).
Axes of the slice: x: 2, y: 2, z: 4, core: 2. Of those that a mesh axis runs over, the one named last changes fastest.
Arguments:
- tokens: bfloat16 [2048, 6144], P('seq'), may hold values from -6 to 6
- qkv_weight: bfloat16 [6144, 3, 1024], P('seq', None, 'dp'), may hold values from -0.078125 to 0.078125
- out_weight: bfloat16 [6144, 1024], P('seq', 'dp'), may hold values from -0.25 to 0.25
- log_decay: float32 [8, 2048], P('dp', 'seq'), may hold values from -1.5 to 0, as said below
- norm_gain: float32 [1024], P('dp'), may hold values from 0.25 to 1.75
Outputs:
- mixed: bfloat16 [2048, 6144], P('seq', 'dp')
The draws below stay inside these ranges and needn't reach their ends.
Inputs may be any that keep to these rules, and one draw needn't show every extreme that they name: `log_decay`: each entry is the logarithm of one head's decay factor at one position.
All inputs are finite; a program needn't handle non-finite values.
Results may differ from the reference program's by a relative error of at most 0.023.
Values may be sent and summed in bfloat16 or wider, within the bound.
A program may use at most 64 MiB of HBM per device.

```python
import math
import jax
import jax.numpy as jnp
from jax import lax

D = 6144
HD = 128
HEADS = 8
TOKENS_PER_SHARD = 256
TOKENS = 2048
N_DP = 4


def draw_log_decay(key, part):
    keys = jax.random.split(jax.random.fold_in(key, 71), 6)
    share_fast = 0.5
    fast = jax.random.uniform(keys[0], (HEADS,), jnp.float32) < share_fast
    fast_rate = jnp.exp(jax.random.uniform(keys[1], (HEADS,), jnp.float32, math.log(1.0 / 50.0), math.log(1.0 / 30.0)))
    slow_decay_rate = jnp.exp(jax.random.uniform(keys[2], (HEADS,), jnp.float32, math.log(0.1), math.log(0.6))) / TOKENS
    rate = jnp.where(fast, fast_rate, slow_decay_rate)
    rough = jax.random.uniform(keys[3], (HEADS, TOKENS), jnp.float32, 0.5, 1.5)
    starting_index = -rate[:, None] * rough
    places = jax.random.randint(keys[4], (HEADS, 2), 0, TOKENS)
    stack_level = jnp.log(jax.random.uniform(keys[5], (HEADS, 2), jnp.float32, 0.5, 0.8))
    aligned_slot = jnp.arange(TOKENS)[None, None, :] == places[:, :, None]
    spike_span = jnp.sum(jnp.where(aligned_slot, stack_level[:, :, None], 0.0), axis=1)
    return (starting_index + spike_span).astype(jnp.float32)


def spiked(array, rng, source, target, blocks, factor):
    def block_of(dim):
        return (jnp.arange(array.shape[dim]) // (array.shape[dim] // blocks)).reshape((-1,) + (1,) * (array.ndim - 1 - dim))

    near = jax.random.permutation(rng, blocks)[block_of(target)]
    far = (block_of(target) + blocks // 2) % blocks
    return jnp.where((block_of(source) == near) | (block_of(source) == far), factor * array, array)


def shard_levels(key, extent, pieces, smallest, largest):
    loudness = 1.0
    for dim, shards_of in pieces:
        steps = jax.random.uniform(jax.random.fold_in(jax.random.fold_in(key, 6), dim), (shards_of,), jnp.float32, smallest / len(pieces), largest / len(pieces))
        loudness = loudness * jnp.repeat(jnp.exp(steps), extent[dim] // shards_of).reshape((-1,) + (1,) * (len(extent) - 1 - dim))
    return loudness


def normal_values(own_key, dims, width, most, shards=(), kind=jnp.bfloat16):
    drawn = width * jax.random.normal(own_key, dims, jnp.float32)
    if shards:
        drawn = drawn * shard_levels(own_key, dims, shards, -0.22, 0.18)
    return jnp.clip(drawn, -most, most).astype(kind)


def bell_draw_with(stream_key, shape, scale, bound, cuts, heavy, dtype=jnp.bfloat16):
    drawn = scale * jax.random.normal(stream_key, shape, jnp.float32)
    if cuts:
        drawn = drawn * shard_levels(stream_key, shape, cuts, -0.22, 0.18)
    return jnp.clip(spiked(drawn, jax.random.fold_in(stream_key, 3), *heavy), -bound, bound).astype(dtype)


def setup_inputs(seed: int = 0) -> dict:
    seeds = jax.random.split(jax.random.key(seed), 6)
    tokens = normal_values(seeds[0], (TOKENS, D), 1.0, 6.0, ((0, 8),))
    qkv_weight = normal_values(seeds[1], (D, 3, HEADS * HD), D ** -0.5, 0.078125, ((0, 8), (2, 4)))
    out_weight = bell_draw_with(seeds[2], (D, HEADS * HD), (HEADS * HD) ** -0.5, 0.25, ((0, 8), (1, 4)), (1, 0, 8, 2.0))
    log_decay = draw_log_decay(jax.random.fold_in(seeds[5], 71), 0)
    norm_gain = jnp.clip(1.0 + 0.15 * jax.random.normal(seeds[4], (HEADS * HD,), jnp.float32), 0.25, 1.75)
    return dict(tokens=tokens, qkv_weight=qkv_weight, out_weight=out_weight, log_decay=log_decay, norm_gain=norm_gain)


def reference(tokens, qkv_weight, out_weight, log_decay, norm_gain):
    blocks = TOKENS // TOKENS_PER_SHARD
    group = HEADS * HD // N_DP
    token_blocks = tokens.reshape(blocks, TOKENS_PER_SHARD, D)
    decay_blocks = jnp.transpose(log_decay.reshape(HEADS, blocks, TOKENS_PER_SHARD), (1, 0, 2))
    flat_qkv = qkv_weight.reshape(D, 3 * HEADS * HD)
    out_groups = out_weight.astype(jnp.float32).reshape(D, N_DP, group)
    gain = norm_gain.reshape(HEADS, HD)
    later = jnp.arange(TOKENS_PER_SHARD)[:, None] >= jnp.arange(TOKENS_PER_SHARD)[None, :]

    def step(state, inputs):
        block_tokens, block_decay = inputs
        proj = jnp.dot(block_tokens, flat_qkv, preferred_element_type=jnp.float32)
        proj = proj.reshape(TOKENS_PER_SHARD, 3, HEADS, HD)
        query = jax.nn.silu(proj[:, 0]).astype(jnp.bfloat16).astype(jnp.float32)
        key = jax.nn.silu(proj[:, 1]).astype(jnp.bfloat16).astype(jnp.float32)
        value = proj[:, 2].astype(jnp.bfloat16).astype(jnp.float32)
        cum = jnp.cumsum(block_decay, axis=1)
        scores = jnp.einsum('thd,shd->hts', query, key)
        spread = cum[:, :, None] - cum[:, None, :]
        factor = jnp.where(later[None], jnp.exp(jnp.minimum(spread, 0.0)), 0.0)
        weights = (scores * factor).astype(jnp.bfloat16).astype(jnp.float32)
        intra = jnp.einsum('hts,shd->thd', weights, value)
        lifted = query * jnp.exp(cum).T[:, :, None]
        inter = jnp.einsum('thd,hde->the', lifted, state, precision=lax.Precision.HIGHEST)
        attn = intra + inter
        scaled_key = (key * jnp.exp(cum[:, -1:] - cum).T[:, :, None]).astype(jnp.bfloat16).astype(jnp.float32)
        local = jnp.einsum('thd,the->hde', scaled_key, value)
        new_state = jnp.exp(cum[:, -1])[:, None, None] * state + local
        power = lax.optimization_barrier(jnp.mean(attn * attn, axis=-1, keepdims=True))
        normalized_output = (attn / jnp.sqrt(power + 1e-05) * gain[None]).astype(jnp.bfloat16)
        normalized_output = normalized_output.astype(jnp.float32).reshape(TOKENS_PER_SHARD, N_DP, group)
        partial_value = jnp.einsum('tng,dng->ntd', normalized_output, out_groups)
        partial_value = partial_value.astype(jnp.bfloat16).astype(jnp.float32)
        mixed = lax.optimization_barrier(jnp.sum(partial_value, axis=0)).astype(jnp.bfloat16)
        return (new_state, mixed)
    start = jnp.zeros((HEADS, HD, HD), jnp.float32)
    final_state, outputs = lax.scan(step, start, (token_blocks, decay_blocks))
    return outputs.reshape(TOKENS, D)
```

```python
import functools

import jax
import jax.numpy as jnp
from jax import lax
from jax.experimental import pallas as pl
from jax.experimental.pallas import tpu as pltpu
from jax.sharding import PartitionSpec as P

MESH = pl.DeviceIdType.MESH
ORDER = (1, 2, 0)


def kernel(
    nz, nd, tok, wqkv, wout, ld, gain, out,
    T, W, G, Wo, Cs, Cr, acc, N, attn, outf, sx_t, sx_r, sl_t, sl_r, dx_t, dx_r, dl_t, dl_r, state,
    loc_sem, t1_s, t1_r, t2_s, t2_r, w_s, w_r, ga_s, ga_r, gb_s, gb_r, c_s, c_r, n_s, n_r,
    sx_s, sx_rs, sl_s, sl_rs, dx_s, dx_rs, dl_s, dl_rs,
):
    d = lax.axis_index("dp")
    s = lax.axis_index("seq")
    z = s // 2
    x = s % 2
    rows = tok.shape[0]
    part = rows // nd
    wide = T.shape[2]
    half = wqkv.shape[1]
    orow, width = wout.shape
    heads, hsize = state.shape[0], state.shape[1]
    f32, bf16 = jnp.float32, jnp.bfloat16

    def dev(dd, zz, xx):
        return (dd, zz * 2 + xx)

    def up(o):
        return lax.rem(z + o, nz)

    def down(o):
        return lax.rem(z + nz - o, nz)

    def dup(o):
        return lax.rem(d + o, nd)

    def ddown(o):
        return lax.rem(d + nd - o, nd)

    def remote(src, dst, ss, rs, to):
        return pltpu.make_async_remote_copy(
            src_ref=src, dst_ref=dst, send_sem=ss, recv_sem=rs, device_id=to, device_id_type=MESH
        )

    def each(lo, hi, f):
        def step(i, carry):
            f(i)
            return carry

        lax.fori_loop(lo, hi, step, 0)

    here = dev(d, z, x)
    across = dev(d, z, 1 - x)
    mine = pl.ds(pl.multiple_of(d * part, part), part)

    barrier = pltpu.get_barrier_semaphore()
    each(1, nz, lambda o: pl.semaphore_signal(barrier, inc=1, device_id=dev(d, up(o), x), device_id_type=MESH))
    each(1, nd, lambda o: pl.semaphore_signal(barrier, inc=1, device_id=dev(dup(o), z, x), device_id_type=MESH))
    each(0, nd, lambda o: pl.semaphore_signal(barrier, inc=1, device_id=dev(dup(o), z, 1 - x), device_id_type=MESH))

    def xrows(xx, n):
        return pl.ds(pl.multiple_of(xx * n, n), n)

    cols = pl.ds(pl.multiple_of(z * wide, wide), wide)
    local_t = pltpu.make_async_copy(tok.at[:, cols], T.at[z], loc_sem.at[0])
    local_w = pltpu.make_async_copy(wqkv, W.at[:, xrows(x, half)], loc_sem.at[1])
    local_g = pltpu.make_async_copy(wout, G.at[z], loc_sem.at[2])
    local_t.start()
    local_w.start()
    local_g.start()
    pl.semaphore_wait(barrier, nz + 2 * nd - 2)

    def t1(o):
        to = pl.ds(pl.multiple_of(up(o) * wide, wide), wide)
        return remote(tok.at[mine, to], T.at[z, mine], t1_s.at[o - 1], t1_r.at[o - 1], dev(d, up(o), x))

    def t2(o, q):
        piece = T.at[down(o), mine]
        return remote(piece, piece, t2_s.at[o - 1, q - 1], t2_r.at[o - 1, q - 1], dev(dup(q), z, x))

    def wx(p):
        return remote(wqkv.at[p], W.at[p, xrows(x, half)], w_s.at[p], w_r.at[p], across)

    def ga(o):
        return remote(wout, G.at[z], ga_s.at[o - 1], ga_r.at[o - 1], dev(d, up(o), x))

    def gb(zz, xx):
        i = x if xx is x else 1 - x
        return remote(G.at[zz], Wo.at[d, xrows(x, orow)], gb_s.at[zz, i], gb_r.at[d, x], dev(zz, z, i))

    def cc(o, p):
        return remote(Cs.at[o - 1, p], Cr.at[o - 1, p], c_s.at[o - 1, p], c_r.at[o - 1, p], dev(d, up(o), x))

    def nn(q):
        return remote(N.at[d], N.at[d], n_s.at[q - 1], n_r.at[q - 1], dev(dup(q), z, x))

    def sl(o):
        return remote(sl_t, sl_r.at[o - 1], sl_s.at[o - 1], sl_rs.at[o - 1], dev(d, up(o), x))

    def dl(o):
        return remote(dl_t, dl_r.at[o - 1], dl_s.at[o - 1], dl_rs.at[o - 1], dev(d, up(o), x))

    sx = remote(sx_t, sx_r, sx_s.at[0], sx_rs.at[0], across)
    dx = remote(dx_t, dx_r, dx_s.at[0], dx_rs.at[0], across)

    each(1, nz, lambda o: t1(o).start())
    for p in ORDER:
        wx(p).start()

    it = lax.broadcasted_iota(jnp.int32, (rows, rows), 0)
    js = lax.broadcasted_iota(jnp.int32, (rows, rows), 1)
    later = it >= js
    cumc, cumr, totals = [], [], []
    for h in range(heads):
        row = ld[h : h + 1, :]
        cumc.append(jnp.sum(jnp.where(later, row, 0.0), axis=1, keepdims=True))
        column = jnp.sum(jnp.where(it == js, row, 0.0), axis=1, keepdims=True)
        cumr.append(jnp.sum(jnp.where(it <= js, column, 0.0), axis=0, keepdims=True))
        totals.append(cumc[h][rows - 1 : rows, :])
        dx_t[h : h + 1, :] = jnp.broadcast_to(totals[h], (1, dx_t.shape[1]))
    for h in range(heads, dx_t.shape[0]):
        dx_t[h : h + 1, :] = jnp.zeros((1, dx_t.shape[1]), f32)
    dx.start()

    def pass_on(o):
        t1(o).wait_recv()
        each(1, nd, lambda q: t2(o, q).start())

    each(1, nz, pass_on)
    each(1, nz, lambda o: ga(o).start())

    dx.wait_recv()
    dl_t[...] = dx_t[...] + dx_r[...]
    each(1, nz, lambda o: dl(o).start())

    local_g.wait()

    def spread(zz):
        gb(zz, None).start()

        @pl.when(zz != d)
        def _():
            gb(zz, x).start()

        @pl.when(zz == d)
        def _():
            pltpu.make_async_copy(G.at[zz], Wo.at[d, xrows(x, orow)], loc_sem.at[3]).start()

    spread(z)
    local_w.wait()
    local_t.wait()

    for p in ORDER:
        wx(p).wait_recv()

        def partial(o, p=p):
            if p == ORDER[0]:
                each(1, nd, lambda q: t2(nz - o, q).wait_recv())
            Cs[o - 1, p] = jnp.dot(T[up(o)], W[p], preferred_element_type=f32).astype(bf16)
            cc(o, p).start()

        each(1, nz, partial)
        acc[p] = jnp.dot(T[z], W[p], preferred_element_type=f32)

    def spread_later(o):
        ga(o).wait_recv()
        spread(down(o))

    each(1, nz, spread_later)

    def whole(p):
        def add(o):
            cc(o, p).wait_recv()
            acc[p] += Cr[o - 1, p].astype(f32)

        each(1, nz, add)
        return acc[p]

    def silu(u):
        return u / (1.0 + jnp.exp(-u))

    key = silu(whole(1)).astype(bf16)
    value = whole(2).astype(bf16)

    def of(a, h):
        return a[:, h * hsize : (h + 1) * hsize]

    def matmul(a, b, dims):
        return lax.dot_general(a, b, (dims, ((), ())), preferred_element_type=f32)

    own = []
    for h in range(heads):
        scaled = (of(key, h).astype(f32) * jnp.exp(totals[h] - cumc[h])).astype(bf16)
        own.append(matmul(scaled, of(value, h), ((0,), (0,))))
        sx_t[h] = own[h].astype(bf16)
    sx.start()

    query = silu(whole(0)).astype(bf16)
    for h in range(heads):
        scores = matmul(of(query, h), of(key, h), ((1,), (1,)))
        factor = jnp.where(later, jnp.exp(jnp.minimum(cumc[h] - cumr[h], 0.0)), 0.0)
        weights = (scores * factor).astype(bf16)
        attn[:, h * hsize : (h + 1) * hsize] = matmul(weights, of(value, h), ((1,), (0,)))

    sx.wait_recv()
    xf = x.astype(f32)
    for h in range(heads):
        other = sx_r[h].astype(f32)
        first = jnp.where(x == 0, own[h], other)
        second = jnp.where(x == 0, other, own[h])
        fall = jnp.exp(jnp.where(x == 0, dx_r[h : h + 1, :], dx_t[h : h + 1, :]))
        sl_t[h] = (fall * first + second).astype(bf16)

    def send_state(o):
        @pl.when(z + o < nz)
        def _():
            sl(o).start()

    each(1, nz, send_state)
    each(1, nz, lambda o: dl(o).wait_recv())
    state[...] = jnp.zeros_like(state)

    def take_state(i):
        o = nz - i

        @pl.when(z - o >= 0)
        def _():
            sl(o).wait_recv()
            for h in range(heads):
                fall = jnp.exp(dl_r[o - 1, h : h + 1, :])
                state[h] = fall * state[h] + sl_r[o - 1, h].astype(f32)

    each(1, nz, take_state)

    @pl.when(x == 1)
    def _():
        for h in range(heads):
            state[h] = jnp.exp(dx_r[h : h + 1, :]) * state[h] + sx_r[h].astype(f32)

    normed = []
    for h in range(heads):
        lifted = of(query, h).astype(f32) * jnp.exp(cumc[h])
        inter = jnp.dot(lifted, state[h], precision=lax.Precision.HIGHEST, preferred_element_type=f32)
        a = attn[:, h * hsize : (h + 1) * hsize] + inter
        power = jnp.mean(a * a, axis=1, keepdims=True)
        g = gain[:, h * hsize : (h + 1) * hsize]
        normed.append((a / jnp.sqrt(power + 1e-05) * g).astype(bf16))
    N[d] = jnp.concatenate(normed, axis=1)
    each(1, nd, lambda q: nn(q).start())

    def arrived(dd, xx):
        remote(G.at[0], Wo.at[dd, xrows(xx, orow)], gb_s.at[0, 0], gb_r.at[dd, xx], across).wait_recv()

    arrived(d, 1 - x)
    pltpu.make_async_copy(G.at[d], Wo.at[d, xrows(x, orow)], loc_sem.at[3]).wait()
    outf[...] = matmul(N[d], Wo[d], ((1,), (1,)))

    def join(q):
        dd = ddown(q)
        nn(q).wait_recv()
        arrived(dd, 0)
        arrived(dd, 1)
        outf[...] += matmul(N[dd], Wo[dd], ((1,), (1,)))

    each(1, nd, join)
    out[...] = outf[...].astype(bf16)

    def sent(o):
        t1(o).wait_send()
        ga(o).wait_send()
        dl(o).wait_send()
        each(1, nd, lambda q: t2(o, q).wait_send())
        for p in ORDER:
            cc(o, p).wait_send()

        @pl.when(z + o < nz)
        def _():
            sl(o).wait_send()

    each(1, nz, sent)
    each(1, nd, lambda q: nn(q).wait_send())
    for p in ORDER:
        wx(p).wait_send()
    sx.wait_send()
    dx.wait_send()

    def left(zz):
        gb(zz, None).wait_send()

        @pl.when(zz != d)
        def _():
            gb(zz, x).wait_send()

    each(0, nz, left)


def body(nz, nd, tokens, qkv_weight, out_weight, log_decay, norm_gain):
    rows, model = tokens.shape
    half, _, width = qkv_weight.shape
    orow = out_weight.shape[0]
    heads = log_decay.shape[0]
    hsize = width // heads
    wide = model // nz
    f32, bf16 = jnp.float32, jnp.bfloat16
    dma = pltpu.SemaphoreType.DMA
    anywhere = pl.BlockSpec(memory_space=pl.ANY)
    vmem = pl.BlockSpec(memory_space=pltpu.VMEM)
    tile = (max(8, heads), hsize)
    flops = 2 * rows * (model * 3 * width + 2 * orow * nd * width)
    return pl.pallas_call(
        functools.partial(kernel, nz, nd),
        out_shape=jax.ShapeDtypeStruct((rows, model // nd), bf16),
        in_specs=[anywhere, anywhere, anywhere, vmem, vmem],
        out_specs=vmem,
        scratch_shapes=[
            pltpu.VMEM((nz, rows, wide), bf16),
            pltpu.VMEM((3, wide, width), bf16),
            pltpu.VMEM((nz, orow, width), bf16),
            pltpu.VMEM((nd, 2 * orow, width), bf16),
            pltpu.VMEM((nz - 1, 3, rows, width), bf16),
            pltpu.VMEM((nz - 1, 3, rows, width), bf16),
            pltpu.VMEM((3, rows, width), f32),
            pltpu.VMEM((nd, rows, width), bf16),
            pltpu.VMEM((rows, width), f32),
            pltpu.VMEM((rows, 2 * orow), f32),
            pltpu.VMEM((heads, hsize, hsize), bf16),
            pltpu.VMEM((heads, hsize, hsize), bf16),
            pltpu.VMEM((heads, hsize, hsize), bf16),
            pltpu.VMEM((nz - 1, heads, hsize, hsize), bf16),
            pltpu.VMEM(tile, f32),
            pltpu.VMEM(tile, f32),
            pltpu.VMEM(tile, f32),
            pltpu.VMEM((nz - 1, *tile), f32),
            pltpu.VMEM((heads, hsize, hsize), f32),
            dma((4,)),
            dma((nz - 1,)), dma((nz - 1,)),
            dma((nz - 1, nd - 1)), dma((nz - 1, nd - 1)),
            dma((3,)), dma((3,)),
            dma((nz - 1,)), dma((nz - 1,)),
            dma((nz, 2)), dma((nd, 2)),
            dma((nz - 1, 3)), dma((nz - 1, 3)),
            dma((nd - 1,)), dma((nd - 1,)),
            dma((1,)), dma((1,)),
            dma((nz - 1,)), dma((nz - 1,)),
            dma((1,)), dma((1,)),
            dma((nz - 1,)), dma((nz - 1,)),
        ],
        compiler_params=pltpu.CompilerParams(
            collective_id=0, has_side_effects=True, vmem_limit_bytes=48 * 2**20
        ),
        cost_estimate=pl.CostEstimate(flops=flops, bytes_accessed=2 * rows * model, transcendentals=0),
    )(tokens, jnp.transpose(qkv_weight, (1, 0, 2)), out_weight, log_decay, norm_gain.reshape(1, width))


def solution(mesh):
    nd = mesh.shape["dp"]
    nz = mesh.shape["seq"] // 2
    assert nz == nd and mesh.shape["seq"] == 2 * nz
    in_specs = (P("seq", None), P("seq", None, "dp"), P("seq", "dp"), P("dp", "seq"), P("dp"))
    return jax.shard_map(
        functools.partial(body, nz, nd), mesh=mesh, in_specs=in_specs, out_specs=P("seq", "dp"), check_vma=False
    )
```

```python
import functools

import jax
import jax.numpy as jnp
from jax import lax
from jax.experimental import pallas as pl
from jax.experimental.pallas import tpu as pltpu
from jax.sharding import PartitionSpec as P

MESH = pl.DeviceIdType.MESH
ORDER = (1, 2, 0)


def kernel(
    nz, nd, tok, wqkv, wout, ld, gain, out,
    T, W, G, Wo, Cs, Cr, P3, N, attn, outf, sx_t, sx_r, sl_t, sl_r, dx_t, dx_r, dl_t, dl_r, state,
    loc_sem, t1_s, t1_r, t2_s, t2_r, w_s, w_r, gu_s, gu_r, gd_s, gd_r, gb_s, gb_r, c_s, c_r, n_s, n_r,
    sx_s, sx_rs, sl_s, sl_rs, dx_s, dx_rs, dl_s, dl_rs,
):
    d = lax.axis_index("dp")
    s = lax.axis_index("seq")
    z = s // 2
    x = s % 2
    rows = tok.shape[0]
    part = rows // nd
    wide = T.shape[2]
    half = wqkv.shape[1]
    orow, width = wout.shape
    heads, hsize = state.shape[0], state.shape[1]
    f32, bf16 = jnp.float32, jnp.bfloat16

    def dev(dd, zz, xx):
        return (dd, zz * 2 + xx)

    def up(o):
        return lax.rem(z + o, nz)

    def down(o):
        return lax.rem(z + nz - o, nz)

    def dup(o):
        return lax.rem(d + o, nd)

    def flip(v, mask):
        bit = 1
        while bit <= mask:
            if mask & bit:
                v = v + bit - 2 * bit * ((v // bit) % 2)
            bit *= 2
        return v

    hops, held, bit = [], [0], nd // 2
    while bit:
        hops.append((bit, list(held)))
        held = held + [m + bit for m in held]
        bit //= 2
    along = [r for r in range(1, nz) if r % 2] + [r for r in range(1, nz) if r % 2 == 0]

    def remote(src, dst, ss, rs, to):
        return pltpu.make_async_remote_copy(
            src_ref=src, dst_ref=dst, send_sem=ss, recv_sem=rs, device_id=to, device_id_type=MESH
        )

    def each(lo, hi, f):
        def step(i, carry):
            f(i)
            return carry

        lax.fori_loop(lo, hi, step, 0)

    here = dev(d, z, x)
    across = dev(d, z, 1 - x)
    mine = pl.ds(pl.multiple_of(d * part, part), part)

    barrier = pltpu.get_barrier_semaphore()
    each(1, nz, lambda o: pl.semaphore_signal(barrier, inc=1, device_id=dev(d, up(o), x), device_id_type=MESH))
    each(1, nd, lambda o: pl.semaphore_signal(barrier, inc=1, device_id=dev(dup(o), z, x), device_id_type=MESH))
    each(0, nd, lambda o: pl.semaphore_signal(barrier, inc=1, device_id=dev(dup(o), z, 1 - x), device_id_type=MESH))

    def xrows(xx, n):
        return pl.ds(pl.multiple_of(xx * n, n), n)

    cols = pl.ds(pl.multiple_of(z * wide, wide), wide)
    local_t = pltpu.make_async_copy(tok.at[:, cols], T.at[z], loc_sem.at[0])
    local_w = pltpu.make_async_copy(wqkv, W.at[:, xrows(x, half)], loc_sem.at[1])
    local_g = pltpu.make_async_copy(wout, G.at[z], loc_sem.at[2])
    local_t.start()
    local_w.start()
    local_g.start()
    pl.semaphore_wait(barrier, nz + 2 * nd - 2)

    def t1(r):
        to = pl.ds(pl.multiple_of(flip(z, r) * wide, wide), wide)
        return remote(tok.at[mine, to], T.at[z, mine], t1_s.at[r - 1], t1_r.at[r - 1], dev(d, flip(z, r), x))

    def t2(r, bit, m):
        piece = T.at[flip(z, r), pl.ds(pl.multiple_of(flip(d, m) * part, part), part)]
        i = m + bit - 1
        return remote(piece, piece, t2_s.at[r - 1, i], t2_r.at[r - 1, i], dev(flip(d, bit), z, x))

    def wx(p):
        return remote(wqkv.at[p], W.at[p, xrows(x, half)], w_s.at[p], w_r.at[p], across)

    def gup(j):
        slot = G.at[z - j]
        return remote(slot, slot, gu_s.at[j], gu_r.at[j], dev(d, z + 1, x))

    def gdown(j):
        slot = G.at[z + j]
        return remote(slot, slot, gd_s.at[j], gd_r.at[j], dev(d, z - 1, x))

    def gb(zz, xx):
        i = x if xx is x else 1 - x
        return remote(G.at[zz], Wo.at[d, xrows(x, orow)], gb_s.at[zz, i], gb_r.at[d, x], dev(zz, z, i))

    def cc(r, p):
        bit = r & -r
        return remote(Cs.at[r - 1, p], Cr.at[r - 1, p], c_s.at[r - 1, p], c_r.at[r - 1, p], dev(d, flip(z, bit), x))

    def nn(bit, m):
        piece = N.at[flip(d, m)]
        i = m + bit - 1
        return remote(piece, piece, n_s.at[i], n_r.at[i], dev(flip(d, bit), z, x))

    def sl(o):
        return remote(sl_t, sl_r.at[o - 1], sl_s.at[o - 1], sl_rs.at[o - 1], dev(d, up(o), x))

    def dl(o):
        return remote(dl_t, dl_r.at[o - 1], dl_s.at[o - 1], dl_rs.at[o - 1], dev(d, up(o), x))

    sx = remote(sx_t, sx_r, sx_s.at[0], sx_rs.at[0], across)
    dx = remote(dx_t, dx_r, dx_s.at[0], dx_rs.at[0], across)

    for r in along:
        t1(r).start()
    for p in ORDER:
        wx(p).start()

    it = lax.broadcasted_iota(jnp.int32, (rows, rows), 0)
    js = lax.broadcasted_iota(jnp.int32, (rows, rows), 1)
    later = it >= js
    cumc, cumr, totals = [], [], []
    for h in range(heads):
        row = ld[h : h + 1, :]
        cumc.append(jnp.sum(jnp.where(later, row, 0.0), axis=1, keepdims=True))
        column = jnp.sum(jnp.where(it == js, row, 0.0), axis=1, keepdims=True)
        cumr.append(jnp.sum(jnp.where(it <= js, column, 0.0), axis=0, keepdims=True))
        totals.append(cumc[h][rows - 1 : rows, :])
        dx_t[h : h + 1, :] = jnp.broadcast_to(totals[h], (1, dx_t.shape[1]))
    for h in range(heads, dx_t.shape[0]):
        dx_t[h : h + 1, :] = jnp.zeros((1, dx_t.shape[1]), f32)
    dx.start()

    for r in along:
        t1(r).wait_recv()
        t2(r, hops[0][0], 0).start()

    def hop(j):
        @pl.when((z - j >= 0) & (z + 1 < nz))
        def _():
            gup(j).start()

        @pl.when((z + j < nz) & (z - 1 >= 0))
        def _():
            gdown(j).start()

    local_g.wait()
    hop(0)

    dx.wait_recv()
    dl_t[...] = dx_t[...] + dx_r[...]
    each(1, nz, lambda o: dl(o).start())

    def spread(zz):
        gb(zz, None).start()

        @pl.when(zz != d)
        def _():
            gb(zz, x).start()

        @pl.when(zz == d)
        def _():
            pltpu.make_async_copy(G.at[zz], Wo.at[d, xrows(x, orow)], loc_sem.at[3]).start()

    spread(z)
    def came(j):
        @pl.when(z - 1 - j >= 0)
        def _():
            remote(G.at[z - 1 - j], G.at[z - 1 - j], gu_s.at[j], gu_r.at[j], here).wait_recv()

        @pl.when(z + 1 + j < nz)
        def _():
            remote(G.at[z + 1 + j], G.at[z + 1 + j], gd_s.at[j], gd_r.at[j], here).wait_recv()

        if j + 1 < nz - 1:
            hop(j + 1)

        @pl.when(z - 1 - j >= 0)
        def _():
            spread(z - 1 - j)

        @pl.when(z + 1 + j < nz)
        def _():
            spread(z + 1 + j)

    local_w.wait()
    local_t.wait()

    for k in range(1, len(hops)):
        before, sent_before = hops[k - 1]
        for r in along:
            for m in sent_before:
                t2(r, before, m).wait_recv()
            for m in hops[k][1]:
                t2(r, hops[k][0], m).start()
    last, sent_last = hops[-1]
    for p in ORDER:
        wx(p).wait_recv()
        for r in along + [0]:
            if p == ORDER[0] and r:
                for m in sent_last:
                    t2(r, last, m).wait_recv()
            product = jnp.dot(T[flip(z, r)], W[p], preferred_element_type=f32)
            if r % 2:
                Cs[r - 1, p] = product.astype(bf16)
                cc(r, p).start()
            else:
                P3[r // 2, p] = product
        if p == ORDER[0]:
            came(0)

    for j in range(1, nz - 2):
        came(j)
    bit = 2
    while bit < nz:
        for p in ORDER:
            for r in list(range(bit, nz, 2 * bit)) + list(range(0, nz, 2 * bit)):
                cc(r + bit // 2, p).wait_recv()
                total = P3[r // 2, p] + Cr[r + bit // 2 - 1, p].astype(f32)
                if r % (2 * bit):
                    Cs[r - 1, p] = total.astype(bf16)
                    cc(r, p).start()
                else:
                    P3[r // 2, p] = total
        bit *= 2
    if nz > 2:
        came(nz - 2)

    def whole(p):
        cc(nz // 2, p).wait_recv()
        return P3[0, p] + Cr[nz // 2 - 1, p].astype(f32)

    def silu(u):
        return u / (1.0 + jnp.exp(-u))

    key = silu(whole(1)).astype(bf16)
    value = whole(2).astype(bf16)

    def of(a, h):
        return a[:, h * hsize : (h + 1) * hsize]

    def matmul(a, b, dims):
        return lax.dot_general(a, b, (dims, ((), ())), preferred_element_type=f32)

    own = []
    for h in range(heads):
        scaled = (of(key, h).astype(f32) * jnp.exp(totals[h] - cumc[h])).astype(bf16)
        own.append(matmul(scaled, of(value, h), ((0,), (0,))))
        sx_t[h] = own[h].astype(bf16)
    sx.start()

    query = silu(whole(0)).astype(bf16)
    for h in range(heads):
        scores = matmul(of(query, h), of(key, h), ((1,), (1,)))
        factor = jnp.where(later, jnp.exp(jnp.minimum(cumc[h] - cumr[h], 0.0)), 0.0)
        weights = (scores * factor).astype(bf16)
        attn[:, h * hsize : (h + 1) * hsize] = matmul(weights, of(value, h), ((1,), (0,)))

    sx.wait_recv()
    xf = x.astype(f32)
    for h in range(heads):
        other = sx_r[h].astype(f32)
        first = jnp.where(x == 0, own[h], other)
        second = jnp.where(x == 0, other, own[h])
        fall = jnp.exp(jnp.where(x == 0, dx_r[h : h + 1, :], dx_t[h : h + 1, :]))
        sl_t[h] = (fall * first + second).astype(bf16)

    def send_state(o):
        @pl.when(z + o < nz)
        def _():
            sl(o).start()

    each(1, nz, send_state)
    each(1, nz, lambda o: dl(o).wait_recv())
    state[...] = jnp.zeros_like(state)

    def take_state(i):
        o = nz - i

        @pl.when(z - o >= 0)
        def _():
            sl(o).wait_recv()
            for h in range(heads):
                fall = jnp.exp(dl_r[o - 1, h : h + 1, :])
                state[h] = fall * state[h] + sl_r[o - 1, h].astype(f32)

    each(1, nz, take_state)

    @pl.when(x == 1)
    def _():
        for h in range(heads):
            state[h] = jnp.exp(dx_r[h : h + 1, :]) * state[h] + sx_r[h].astype(f32)

    normed = []
    for h in range(heads):
        lifted = of(query, h).astype(f32) * jnp.exp(cumc[h])
        inter = jnp.dot(lifted, state[h], precision=lax.Precision.HIGHEST, preferred_element_type=f32)
        a = attn[:, h * hsize : (h + 1) * hsize] + inter
        power = jnp.mean(a * a, axis=1, keepdims=True)
        g = gain[:, h * hsize : (h + 1) * hsize]
        normed.append((a / jnp.sqrt(power + 1e-05) * g).astype(bf16))
    N[d] = jnp.concatenate(normed, axis=1)
    nn(hops[0][0], 0).start()

    def arrived(dd, xx):
        remote(G.at[0], Wo.at[dd, xrows(xx, orow)], gb_s.at[0, 0], gb_r.at[dd, xx], across).wait_recv()

    arrived(d, 1 - x)
    pltpu.make_async_copy(G.at[d], Wo.at[d, xrows(x, orow)], loc_sem.at[3]).wait()
    outf[...] = matmul(N[d], Wo[d], ((1,), (1,)))

    for k, (bit, pieces) in enumerate(hops):
        for m in pieces:
            nn(bit, m).wait_recv()
        if k + 1 < len(hops):
            for m in hops[k + 1][1]:
                nn(hops[k + 1][0], m).start()
        for m in pieces:
            dd = flip(d, m + bit)
            arrived(dd, 0)
            arrived(dd, 1)
            outf[...] += matmul(N[dd], Wo[dd], ((1,), (1,)))

    out[...] = outf[...].astype(bf16)

    def sent(o):
        dl(o).wait_send()

        @pl.when(z + o < nz)
        def _():
            sl(o).wait_send()

    each(1, nz, sent)
    for r in along:
        t1(r).wait_send()
        for bit, pieces in hops:
            for m in pieces:
                t2(r, bit, m).wait_send()
        for p in ORDER:
            cc(r, p).wait_send()
    for bit, pieces in hops:
        for m in pieces:
            nn(bit, m).wait_send()
    for j in range(nz - 1):

        @pl.when((z - j >= 0) & (z + 1 < nz))
        def _(j=j):
            gup(j).wait_send()

        @pl.when((z + j < nz) & (z - 1 >= 0))
        def _(j=j):
            gdown(j).wait_send()

    for p in ORDER:
        wx(p).wait_send()
    sx.wait_send()
    dx.wait_send()

    def left(zz):
        gb(zz, None).wait_send()

        @pl.when(zz != d)
        def _():
            gb(zz, x).wait_send()

    each(0, nz, left)


def body(nz, nd, tokens, qkv_weight, out_weight, log_decay, norm_gain):
    rows, model = tokens.shape
    half, _, width = qkv_weight.shape
    orow = out_weight.shape[0]
    heads = log_decay.shape[0]
    hsize = width // heads
    wide = model // nz
    f32, bf16 = jnp.float32, jnp.bfloat16
    dma = pltpu.SemaphoreType.DMA
    anywhere = pl.BlockSpec(memory_space=pl.ANY)
    vmem = pl.BlockSpec(memory_space=pltpu.VMEM)
    tile = (max(8, heads), hsize)
    flops = 2 * rows * (model * 3 * width + 2 * orow * nd * width)
    return pl.pallas_call(
        functools.partial(kernel, nz, nd),
        out_shape=jax.ShapeDtypeStruct((rows, model // nd), bf16),
        in_specs=[anywhere, anywhere, anywhere, vmem, vmem],
        out_specs=vmem,
        scratch_shapes=[
            pltpu.VMEM((nz, rows, wide), bf16),
            pltpu.VMEM((3, wide, width), bf16),
            pltpu.VMEM((nz, orow, width), bf16),
            pltpu.VMEM((nd, 2 * orow, width), bf16),
            pltpu.VMEM((nz - 1, 3, rows, width), bf16),
            pltpu.VMEM((nz - 1, 3, rows, width), bf16),
            pltpu.VMEM((nz // 2, 3, rows, width), f32),
            pltpu.VMEM((nd, rows, width), bf16),
            pltpu.VMEM((rows, width), f32),
            pltpu.VMEM((rows, 2 * orow), f32),
            pltpu.VMEM((heads, hsize, hsize), bf16),
            pltpu.VMEM((heads, hsize, hsize), bf16),
            pltpu.VMEM((heads, hsize, hsize), bf16),
            pltpu.VMEM((nz - 1, heads, hsize, hsize), bf16),
            pltpu.VMEM(tile, f32),
            pltpu.VMEM(tile, f32),
            pltpu.VMEM(tile, f32),
            pltpu.VMEM((nz - 1, *tile), f32),
            pltpu.VMEM((heads, hsize, hsize), f32),
            dma((4,)),
            dma((nz - 1,)), dma((nz - 1,)),
            dma((nz - 1, nd - 1)), dma((nz - 1, nd - 1)),
            dma((3,)), dma((3,)),
            dma((nz - 1,)), dma((nz - 1,)),
            dma((nz - 1,)), dma((nz - 1,)),
            dma((nz, 2)), dma((nd, 2)),
            dma((nz - 1, 3)), dma((nz - 1, 3)),
            dma((nd - 1,)), dma((nd - 1,)),
            dma((1,)), dma((1,)),
            dma((nz - 1,)), dma((nz - 1,)),
            dma((1,)), dma((1,)),
            dma((nz - 1,)), dma((nz - 1,)),
        ],
        compiler_params=pltpu.CompilerParams(
            collective_id=0, has_side_effects=True, vmem_limit_bytes=61 * 2**20
        ),
        cost_estimate=pl.CostEstimate(flops=flops, bytes_accessed=2 * rows * model, transcendentals=0),
    )(tokens, jnp.transpose(qkv_weight, (1, 0, 2)), out_weight, log_decay, norm_gain.reshape(1, width))


def solution(mesh):
    nd = mesh.shape["dp"]
    nz = mesh.shape["seq"] // 2
    assert nz == nd and nz & (nz - 1) == 0 and nz > 1 and mesh.shape["seq"] == 2 * nz
    in_specs = (P("seq", None), P("seq", None, "dp"), P("seq", "dp"), P("dp", "seq"), P("dp"))
    return jax.shard_map(
        functools.partial(body, nz, nd), mesh=mesh, in_specs=in_specs, out_specs=P("seq", "dp"), check_vma=False
    )
```

```python
import functools

import jax
import jax.numpy as jnp
from jax import lax
from jax.experimental import pallas as pl
from jax.experimental.pallas import tpu as pltpu
from jax.sharding import PartitionSpec as P

MESH = pl.DeviceIdType.MESH
ORDER = (1, 2, 0)


def kernel(
    nz, nd, tok, wqkv, wout, ld, gain, out,
    T, W, G, Wo, Cs, Cr, P3, N, attn, outf, sx_t, sx_r, sl_t, sl_r, dx_t, dx_r, dl_t, dl_r, state,
    loc_sem, t1_s, t1_r, t2_s, t2_r, w_s, w_r, gu_s, gu_r, gd_s, gd_r, gb_s, gb_r, c_s, c_r, n_s, n_r,
    sx_s, sx_rs, sl_s, sl_rs, dx_s, dx_rs, dl_s, dl_rs,
):
    d = lax.axis_index("dp")
    s = lax.axis_index("seq")
    z = s // 2
    x = s % 2
    rows = tok.shape[0]
    part = rows // nd
    wide = T.shape[2]
    half = wqkv.shape[1]
    orow, width = wout.shape
    heads, hsize = state.shape[0], state.shape[1]
    f32, bf16 = jnp.float32, jnp.bfloat16

    def dev(dd, zz, xx):
        return (dd, zz * 2 + xx)

    def up(o):
        return lax.rem(z + o, nz)

    def down(o):
        return lax.rem(z + nz - o, nz)

    def dup(o):
        return lax.rem(d + o, nd)

    def flip(v, mask):
        bit = 1
        while bit <= mask:
            if mask & bit:
                v = v + bit - 2 * bit * ((v // bit) % 2)
            bit *= 2
        return v

    hops, held, bit = [], [0], nd // 2
    while bit:
        hops.append((bit, list(held)))
        held = held + [m + bit for m in held]
        bit //= 2
    along = [r for r in range(1, nz) if r % 2] + [r for r in range(1, nz) if r % 2 == 0]

    def remote(src, dst, ss, rs, to):
        return pltpu.make_async_remote_copy(
            src_ref=src, dst_ref=dst, send_sem=ss, recv_sem=rs, device_id=to, device_id_type=MESH
        )

    def each(lo, hi, f):
        def step(i, carry):
            f(i)
            return carry

        lax.fori_loop(lo, hi, step, 0)

    here = dev(d, z, x)
    across = dev(d, z, 1 - x)
    mine = pl.ds(pl.multiple_of(d * part, part), part)

    barrier = pltpu.get_barrier_semaphore()
    each(1, nz, lambda o: pl.semaphore_signal(barrier, inc=1, device_id=dev(d, up(o), x), device_id_type=MESH))
    each(1, nd, lambda o: pl.semaphore_signal(barrier, inc=1, device_id=dev(dup(o), z, x), device_id_type=MESH))
    each(0, nd, lambda o: pl.semaphore_signal(barrier, inc=1, device_id=dev(dup(o), z, 1 - x), device_id_type=MESH))

    def xrows(xx, n):
        return pl.ds(pl.multiple_of(xx * n, n), n)

    cols = pl.ds(pl.multiple_of(z * wide, wide), wide)
    local_t = pltpu.make_async_copy(tok.at[:, cols], T.at[z], loc_sem.at[0])
    local_w = pltpu.make_async_copy(wqkv, W.at[:, xrows(x, half)], loc_sem.at[1])
    local_g = pltpu.make_async_copy(wout, G.at[z], loc_sem.at[2])
    local_t.start()
    local_w.start()
    local_g.start()
    pl.semaphore_wait(barrier, nz + 2 * nd - 2)

    def t1(r):
        to = pl.ds(pl.multiple_of(flip(z, r) * wide, wide), wide)
        return remote(tok.at[mine, to], T.at[z, mine], t1_s.at[r - 1], t1_r.at[r - 1], dev(d, flip(z, r), x))

    def t2(r, bit, m):
        piece = T.at[flip(z, r), pl.ds(pl.multiple_of(flip(d, m) * part, part), part)]
        i = m + bit - 1
        return remote(piece, piece, t2_s.at[r - 1, i], t2_r.at[r - 1, i], dev(flip(d, bit), z, x))

    def wx(p):
        return remote(wqkv.at[p], W.at[p, xrows(x, half)], w_s.at[p], w_r.at[p], across)

    def gup(j):
        slot = G.at[z - j]
        return remote(slot, slot, gu_s.at[j], gu_r.at[j], dev(d, z + 1, x))

    def gdown(j):
        slot = G.at[z + j]
        return remote(slot, slot, gd_s.at[j], gd_r.at[j], dev(d, z - 1, x))

    def gb(zz, xx):
        i = x if xx is x else 1 - x
        return remote(G.at[zz], Wo.at[d, xrows(x, orow)], gb_s.at[zz, i], gb_r.at[d, x], dev(zz, z, i))

    def cc(r, p):
        bit = r & -r
        return remote(Cs.at[r - 1, p], Cr.at[r - 1, p], c_s.at[r - 1, p], c_r.at[r - 1, p], dev(d, flip(z, bit), x))

    def nn(bit, m):
        piece = N.at[flip(d, m)]
        i = m + bit - 1
        return remote(piece, piece, n_s.at[i], n_r.at[i], dev(flip(d, bit), z, x))

    def sl(o):
        return remote(sl_t, sl_r.at[o - 1], sl_s.at[o - 1], sl_rs.at[o - 1], dev(d, up(o), x))

    def dl(o):
        return remote(dl_t, dl_r.at[o - 1], dl_s.at[o - 1], dl_rs.at[o - 1], dev(d, up(o), x))

    sx = remote(sx_t, sx_r, sx_s.at[0], sx_rs.at[0], across)
    dx = remote(dx_t, dx_r, dx_s.at[0], dx_rs.at[0], across)

    def hop(j):
        @pl.when((z - j >= 0) & (z + 1 < nz))
        def _():
            gup(j).start()

        @pl.when((z + j < nz) & (z - 1 >= 0))
        def _():
            gdown(j).start()


    for r in along:
        t1(r).start()
    for p in ORDER:
        wx(p).start()
    local_g.wait()
    hop(0)

    it = lax.broadcasted_iota(jnp.int32, (rows, rows), 0)
    js = lax.broadcasted_iota(jnp.int32, (rows, rows), 1)
    later = it >= js
    cumc, cumr, totals = [], [], []
    for h in range(heads):
        row = ld[h : h + 1, :]
        cumc.append(jnp.sum(jnp.where(later, row, 0.0), axis=1, keepdims=True))
        column = jnp.sum(jnp.where(it == js, row, 0.0), axis=1, keepdims=True)
        cumr.append(jnp.sum(jnp.where(it <= js, column, 0.0), axis=0, keepdims=True))
        totals.append(cumc[h][rows - 1 : rows, :])
        dx_t[h : h + 1, :] = jnp.broadcast_to(totals[h], (1, dx_t.shape[1]))
    for h in range(heads, dx_t.shape[0]):
        dx_t[h : h + 1, :] = jnp.zeros((1, dx_t.shape[1]), f32)
    dx.start()

    for r in along:
        t1(r).wait_recv()
        t2(r, hops[0][0], 0).start()


    dx.wait_recv()
    dl_t[...] = dx_t[...] + dx_r[...]
    each(1, nz, lambda o: dl(o).start())

    def spread(zz):
        gb(zz, None).start()

        @pl.when(zz != d)
        def _():
            gb(zz, x).start()

        @pl.when(zz == d)
        def _():
            pltpu.make_async_copy(G.at[zz], Wo.at[d, xrows(x, orow)], loc_sem.at[3]).start()

    spread(z)
    def came(j):
        @pl.when(z - 1 - j >= 0)
        def _():
            remote(G.at[z - 1 - j], G.at[z - 1 - j], gu_s.at[j], gu_r.at[j], here).wait_recv()

        @pl.when(z + 1 + j < nz)
        def _():
            remote(G.at[z + 1 + j], G.at[z + 1 + j], gd_s.at[j], gd_r.at[j], here).wait_recv()

        if j + 1 < nz - 1:
            hop(j + 1)

        @pl.when(z - 1 - j >= 0)
        def _():
            spread(z - 1 - j)

        @pl.when(z + 1 + j < nz)
        def _():
            spread(z + 1 + j)

    local_w.wait()
    local_t.wait()

    for k in range(1, len(hops)):
        before, sent_before = hops[k - 1]
        for r in along:
            for m in sent_before:
                t2(r, before, m).wait_recv()
            for m in hops[k][1]:
                t2(r, hops[k][0], m).start()
    last, sent_last = hops[-1]
    came(0)
    for p in ORDER:
        wx(p).wait_recv()
        for r in along + [0]:
            if p == ORDER[0] and r:
                for m in sent_last:
                    t2(r, last, m).wait_recv()
            product = jnp.dot(T[flip(z, r)], W[p], preferred_element_type=f32)
            if r % 2:
                Cs[r - 1, p] = product.astype(bf16)
                cc(r, p).start()
            else:
                P3[r // 2, p] = product
        if p == ORDER[0] and nz > 2:
            came(1)

    for j in range(2, nz - 1):
        came(j)
    bit = 2
    while bit < nz:
        for p in ORDER:
            for r in list(range(bit, nz, 2 * bit)) + list(range(0, nz, 2 * bit)):
                cc(r + bit // 2, p).wait_recv()
                total = P3[r // 2, p] + Cr[r + bit // 2 - 1, p].astype(f32)
                if r % (2 * bit):
                    Cs[r - 1, p] = total.astype(bf16)
                    cc(r, p).start()
                else:
                    P3[r // 2, p] = total
        bit *= 2

    def whole(p):
        cc(nz // 2, p).wait_recv()
        return P3[0, p] + Cr[nz // 2 - 1, p].astype(f32)

    def silu(u):
        return u / (1.0 + jnp.exp(-u))

    key = silu(whole(1)).astype(bf16)
    value = whole(2).astype(bf16)

    def of(a, h):
        return a[:, h * hsize : (h + 1) * hsize]

    def matmul(a, b, dims):
        return lax.dot_general(a, b, (dims, ((), ())), preferred_element_type=f32)

    own = []
    for h in range(heads):
        scaled = (of(key, h).astype(f32) * jnp.exp(totals[h] - cumc[h])).astype(bf16)
        own.append(matmul(scaled, of(value, h), ((0,), (0,))))
        sx_t[h] = own[h].astype(bf16)
    sx.start()

    query = silu(whole(0)).astype(bf16)
    for h in range(heads):
        scores = matmul(of(query, h), of(key, h), ((1,), (1,)))
        factor = jnp.where(later, jnp.exp(jnp.minimum(cumc[h] - cumr[h], 0.0)), 0.0)
        weights = (scores * factor).astype(bf16)
        attn[:, h * hsize : (h + 1) * hsize] = matmul(weights, of(value, h), ((1,), (0,)))

    sx.wait_recv()
    xf = x.astype(f32)
    for h in range(heads):
        other = sx_r[h].astype(f32)
        first = jnp.where(x == 0, own[h], other)
        second = jnp.where(x == 0, other, own[h])
        fall = jnp.exp(jnp.where(x == 0, dx_r[h : h + 1, :], dx_t[h : h + 1, :]))
        sl_t[h] = (fall * first + second).astype(bf16)

    def send_state(o):
        @pl.when(z + o < nz)
        def _():
            sl(o).start()

    each(1, nz, send_state)
    each(1, nz, lambda o: dl(o).wait_recv())
    state[...] = jnp.zeros_like(state)

    def take_state(i):
        o = nz - i

        @pl.when(z - o >= 0)
        def _():
            sl(o).wait_recv()
            for h in range(heads):
                fall = jnp.exp(dl_r[o - 1, h : h + 1, :])
                state[h] = fall * state[h] + sl_r[o - 1, h].astype(f32)

    each(1, nz, take_state)

    @pl.when(x == 1)
    def _():
        for h in range(heads):
            state[h] = jnp.exp(dx_r[h : h + 1, :]) * state[h] + sx_r[h].astype(f32)

    normed = []
    for h in range(heads):
        lifted = of(query, h).astype(f32) * jnp.exp(cumc[h])
        inter = jnp.dot(lifted, state[h], precision=lax.Precision.HIGHEST, preferred_element_type=f32)
        a = attn[:, h * hsize : (h + 1) * hsize] + inter
        power = jnp.mean(a * a, axis=1, keepdims=True)
        g = gain[:, h * hsize : (h + 1) * hsize]
        normed.append((a / jnp.sqrt(power + 1e-05) * g).astype(bf16))
    N[d] = jnp.concatenate(normed, axis=1)
    nn(hops[0][0], 0).start()

    def arrived(dd, xx):
        remote(G.at[0], Wo.at[dd, xrows(xx, orow)], gb_s.at[0, 0], gb_r.at[dd, xx], across).wait_recv()

    arrived(d, 1 - x)
    pltpu.make_async_copy(G.at[d], Wo.at[d, xrows(x, orow)], loc_sem.at[3]).wait()
    outf[...] = matmul(N[d], Wo[d], ((1,), (1,)))

    for k, (bit, pieces) in enumerate(hops):
        for m in pieces:
            nn(bit, m).wait_recv()
        if k + 1 < len(hops):
            for m in hops[k + 1][1]:
                nn(hops[k + 1][0], m).start()
        for m in pieces:
            dd = flip(d, m + bit)
            arrived(dd, 0)
            arrived(dd, 1)
            outf[...] += matmul(N[dd], Wo[dd], ((1,), (1,)))

    out[...] = outf[...].astype(bf16)

    def sent(o):
        dl(o).wait_send()

        @pl.when(z + o < nz)
        def _():
            sl(o).wait_send()

    each(1, nz, sent)
    for r in along:
        t1(r).wait_send()
        for bit, pieces in hops:
            for m in pieces:
                t2(r, bit, m).wait_send()
        for p in ORDER:
            cc(r, p).wait_send()
    for bit, pieces in hops:
        for m in pieces:
            nn(bit, m).wait_send()
    for j in range(nz - 1):

        @pl.when((z - j >= 0) & (z + 1 < nz))
        def _(j=j):
            gup(j).wait_send()

        @pl.when((z + j < nz) & (z - 1 >= 0))
        def _(j=j):
            gdown(j).wait_send()

    for p in ORDER:
        wx(p).wait_send()
    sx.wait_send()
    dx.wait_send()

    def left(zz):
        gb(zz, None).wait_send()

        @pl.when(zz != d)
        def _():
            gb(zz, x).wait_send()

    each(0, nz, left)


def body(nz, nd, tokens, qkv_weight, out_weight, log_decay, norm_gain):
    rows, model = tokens.shape
    half, _, width = qkv_weight.shape
    orow = out_weight.shape[0]
    heads = log_decay.shape[0]
    hsize = width // heads
    wide = model // nz
    f32, bf16 = jnp.float32, jnp.bfloat16
    dma = pltpu.SemaphoreType.DMA
    anywhere = pl.BlockSpec(memory_space=pl.ANY)
    vmem = pl.BlockSpec(memory_space=pltpu.VMEM)
    tile = (max(8, heads), hsize)
    flops = 2 * rows * (model * 3 * width + 2 * orow * nd * width)
    return pl.pallas_call(
        functools.partial(kernel, nz, nd),
        out_shape=jax.ShapeDtypeStruct((rows, model // nd), bf16),
        in_specs=[anywhere, anywhere, anywhere, vmem, vmem],
        out_specs=vmem,
        scratch_shapes=[
            pltpu.VMEM((nz, rows, wide), bf16),
            pltpu.VMEM((3, wide, width), bf16),
            pltpu.VMEM((nz, orow, width), bf16),
            pltpu.VMEM((nd, 2 * orow, width), bf16),
            pltpu.VMEM((nz - 1, 3, rows, width), bf16),
            pltpu.VMEM((nz - 1, 3, rows, width), bf16),
            pltpu.VMEM((nz // 2, 3, rows, width), f32),
            pltpu.VMEM((nd, rows, width), bf16),
            pltpu.VMEM((rows, width), f32),
            pltpu.VMEM((rows, 2 * orow), f32),
            pltpu.VMEM((heads, hsize, hsize), bf16),
            pltpu.VMEM((heads, hsize, hsize), bf16),
            pltpu.VMEM((heads, hsize, hsize), bf16),
            pltpu.VMEM((nz - 1, heads, hsize, hsize), bf16),
            pltpu.VMEM(tile, f32),
            pltpu.VMEM(tile, f32),
            pltpu.VMEM(tile, f32),
            pltpu.VMEM((nz - 1, *tile), f32),
            pltpu.VMEM((heads, hsize, hsize), f32),
            dma((4,)),
            dma((nz - 1,)), dma((nz - 1,)),
            dma((nz - 1, nd - 1)), dma((nz - 1, nd - 1)),
            dma((3,)), dma((3,)),
            dma((nz - 1,)), dma((nz - 1,)),
            dma((nz - 1,)), dma((nz - 1,)),
            dma((nz, 2)), dma((nd, 2)),
            dma((nz - 1, 3)), dma((nz - 1, 3)),
            dma((nd - 1,)), dma((nd - 1,)),
            dma((1,)), dma((1,)),
            dma((nz - 1,)), dma((nz - 1,)),
            dma((1,)), dma((1,)),
            dma((nz - 1,)), dma((nz - 1,)),
        ],
        compiler_params=pltpu.CompilerParams(
            collective_id=0, has_side_effects=True, vmem_limit_bytes=61 * 2**20
        ),
        cost_estimate=pl.CostEstimate(flops=flops, bytes_accessed=2 * rows * model, transcendentals=0),
    )(tokens, jnp.transpose(qkv_weight, (1, 0, 2)), out_weight, log_decay, norm_gain.reshape(1, width))


def solution(mesh):
    nd = mesh.shape["dp"]
    nz = mesh.shape["seq"] // 2
    assert nz == nd and nz & (nz - 1) == 0 and nz > 1 and mesh.shape["seq"] == 2 * nz
    in_specs = (P("seq", None), P("seq", None, "dp"), P("seq", "dp"), P("dp", "seq"), P("dp"))
    return jax.shard_map(
        functools.partial(body, nz, nd), mesh=mesh, in_specs=in_specs, out_specs=P("seq", "dp"), check_vma=False
    )
```
